32 devices in a mesh: parts: 2 (over x), blk: 16 (over z, y, core).
Axes of the slice: x: 2, y: 2, z: 4, core: 2. Of those that a mesh axis runs over, the one named last changes fastest.
Arguments:
- small_emb: bfloat16 [8192, 768], P(('parts', 'blk')), parts along dimension 0
- small_cluster: int32 [8192], P(('parts', 'blk')), parts along dimension 0, may hold values from 0 to 255, as said below
- small_index: int32 [8192], P(('parts', 'blk')), parts along dimension 0, may hold values from 0 to 4095, each once
- big_emb: bfloat16 [16384, 768], P(('parts', 'blk')), parts along dimension 0
- big_cluster: int32 [16384], P(('parts', 'blk')), parts along dimension 0, may hold values from 0 to 1, as said below
- big_index: int32 [16384], P(('parts', 'blk')), parts along dimension 0, may hold values from 0 to 8191, each once
Outputs:
- small_best: float32 [8192], P(('parts', 'blk')), parts along dimension 0
- big_best: float32 [16384], P(('parts', 'blk')), parts along dimension 0
The draws below stay inside these ranges and needn't reach their ends.
There are 2 independent parts, one for each index of `parts`. The reference program is written for one: setup_inputs(seed, part) draws one part's arguments, and reference() takes and returns one part's arrays. A program takes and returns all parts, laid end to end along the dimension named above; each array names one. Nothing has to cross between parts.
Inputs may be any that keep to these rules, and one draw needn't show every extreme that they name: `small_cluster`: on every device, at most 32 rows carry ids with one remainder on division by 16; on every device some remainder is held by exactly 32 rows, and one remainder is held by 32 rows on every device. `big_cluster`: rows on the devices with blk indices g * 16 to (g + 1) * 16 - 1 carry ids g * 2 to (g + 1) * 2 - 1.
All inputs are finite; a program needn't handle non-finite values.
Results may differ from the reference program's by a relative error of at most 0.00051.
Values may be sent and summed in bfloat16 or wider, within the bound.
A program may use at most 64 MiB of HBM per device.

```python
import math
import jax
import jax.numpy as jnp
from jax import lax

D = 768
ROWS_DEV = 256
CL_OWN = 16
BIG_DEV = 512
CYCLE = 16
BIGS = 2
CAP = 32
SMALL = 4096
CLUSTERS = 256
BIG = 8192
BIG_CLUSTERS = 2
N_BLK = 16


def small_layout(key):
    blocks = SMALL // ROWS_DEV
    position_count = blocks * CAP
    key_list = jax.random.split(key, 6)
    holder_weight = jax.random.randint(key_list[0], (blocks,), 0, 3)
    preferred_pick = jax.random.randint(key_list[1], (), 0, blocks)
    selected_slot = jax.random.randint(key_list[2], (blocks,), 0, blocks)
    random_noise_bits = jax.random.randint(key_list[3], (blocks, position_count), 0, 4096)
    position_ids = jnp.arange(position_count, dtype=jnp.int32)
    position_holder = position_ids // CAP
    reward_extra = holder_weight[position_holder][None, :] + 8 * (position_holder[None, :] == preferred_pick) + 8 * (position_holder[None, :] == selected_slot[:, None])
    slot_scores = (reward_extra * 4096 + random_noise_bits) * position_count + position_ids[None, :]
    picked = lax.top_k(slot_scores, ROWS_DEV)[1]
    target = picked // CAP
    member = jax.random.randint(key_list[4], (blocks, ROWS_DEV), 0, CL_OWN)
    cluster_ids = target + blocks * member

    def shuffle_one(row_key):
        return jax.random.permutation(row_key, ROWS_DEV)
    orders = jax.vmap(shuffle_one)(jax.random.split(key_list[5], blocks))
    cluster_ids = jnp.take_along_axis(cluster_ids, orders, axis=1)
    return cluster_ids.reshape(SMALL).astype(jnp.int32)


def big_layout(key):
    group_rows = CYCLE * BIG_DEV
    key_list = jax.random.split(key, 3)
    row_ids = jnp.arange(BIG, dtype=jnp.int32)
    group_of = row_ids // group_rows
    base_ids = group_of * BIGS + jax.random.randint(key_list[0], (BIG,), 0, BIGS)
    partner = group_of * group_rows + jax.random.randint(key_list[1], (BIG,), 0, group_rows)
    copied = jax.random.randint(key_list[2], (BIG,), 0, 4) == 0
    final_ids = jnp.where(copied, base_ids[partner], base_ids)
    return (base_ids, partner, copied, final_ids)


def row_noise(key, count, spread):
    key_list = jax.random.split(key, 4)
    noise_rows = jax.random.normal(key_list[0], (count, D), jnp.float32)
    scales = jnp.exp(jax.random.uniform(key_list[1], (count, 1), jnp.float32, 0.0, math.log(10.0)))
    extra = spread * jax.random.normal(key_list[3], (count, D), jnp.float32)
    return (noise_rows, scales, extra)


def draw_small_cluster(key, part):
    return small_layout(key)


def draw_small_emb(key, part):
    cluster_ids = small_layout(key)
    key = jax.random.fold_in(key, 21)
    center_key, noise_key = jax.random.split(key)
    centers = jax.random.normal(center_key, (CLUSTERS, D), jnp.float32)
    noise_rows, scales, extra = row_noise(noise_key, SMALL, 0.0)
    values = (0.8 * centers[cluster_ids] + noise_rows) * scales
    return values.astype(jnp.bfloat16)


def draw_big_cluster(key, part):
    return big_layout(key)[3].astype(jnp.int32)


def draw_big_emb(key, part):
    base_ids, partner, copied, final_ids = big_layout(key)
    key = jax.random.fold_in(key, 33)
    center_key, noise_key = jax.random.split(key)
    centers = jax.random.normal(center_key, (BIG_CLUSTERS, D), jnp.float32)
    noise_rows, scales, extra = row_noise(noise_key, BIG, 0.25)
    base_rows = 0.8 * centers[base_ids] + noise_rows
    values = jnp.where(copied[:, None], base_rows[partner] + extra, base_rows) * scales
    return values.astype(jnp.bfloat16)


def setup_inputs(seed: int = 0, part: int = 0) -> dict:
    key_of = jax.random.split(jax.random.key(seed), 7)
    part_keys = jax.random.split(jax.random.fold_in(key_of[6], part), 7)
    return {
        "small_emb": draw_small_emb(jax.random.fold_in(jax.random.fold_in(key_of[6], part), 71), part),
        "small_cluster": draw_small_cluster(jax.random.fold_in(jax.random.fold_in(key_of[6], part), 71), part),
        "small_index": jax.random.permutation(part_keys[2], SMALL).astype(jnp.int32),
        "big_emb": draw_big_emb(jax.random.fold_in(jax.random.fold_in(key_of[6], part), 71), part),
        "big_cluster": draw_big_cluster(jax.random.fold_in(jax.random.fold_in(key_of[6], part), 71), part),
        "big_index": jax.random.permutation(part_keys[5], BIG).astype(jnp.int32),
    }


def unit_rows(matrix):
    widened = matrix.astype(jnp.float32)
    scaled = widened * lax.rsqrt(lax.optimization_barrier(jnp.sum(widened * widened, axis=1, keepdims=True)) + 1e-06)
    return scaled.astype(jnp.bfloat16)

def masked_best(queries, query_ids, query_order, keys_in, key_ids, key_order):
    sim_grid = jnp.dot(queries.astype(jnp.float32), keys_in.astype(jnp.float32).T, preferred_element_type=jnp.float32)
    keep_mask = (query_ids[:, None] == key_ids[None, :]) & (key_order[None, :] < query_order[:, None])
    return lax.optimization_barrier(jnp.max(jnp.where(keep_mask, sim_grid, -1.0), axis=1))

def reference(small_emb, small_cluster, small_index, big_emb, big_cluster, big_index):
    small_unit = unit_rows(small_emb)
    position_count = 2 * ROWS_DEV
    owner_of = small_cluster % N_BLK
    pad_unit = jnp.concatenate([small_unit, jnp.zeros((1, D), jnp.bfloat16)], axis=0)
    pad_ids = jnp.concatenate([small_cluster, jnp.full((1,), -1, jnp.int32)], axis=0)
    pad_order = jnp.concatenate([small_index, jnp.zeros((1,), jnp.int32)], axis=0)

    def per_owner(owner):
        places = jnp.nonzero(owner_of == owner, size=position_count, fill_value=SMALL)[0]
        members = pad_unit[places]
        member_ids = pad_ids[places]
        member_order = pad_order[places]
        return (masked_best(members, member_ids, member_order, members, member_ids, member_order), places)
    values, places = lax.map(per_owner, jnp.arange(N_BLK, dtype=jnp.int32))
    small_best = jnp.full((SMALL + 1,), -1.0, jnp.float32).at[places.reshape(-1)].set(values.reshape(-1))[:SMALL]
    big_unit = unit_rows(big_emb)
    group_rows = CYCLE * BIG_DEV
    groups = BIG // group_rows
    grouped = (big_unit.reshape(groups, group_rows, D), big_cluster.reshape(groups, group_rows), big_index.reshape(groups, group_rows))

    def per_group(members):
        member_unit, member_ids, member_order = members

        def per_block(block_num):
            start = block_num * BIG_DEV
            queries = lax.dynamic_slice_in_dim(member_unit, start, BIG_DEV, 0)
            query_ids = lax.dynamic_slice_in_dim(member_ids, start, BIG_DEV, 0)
            query_order = lax.dynamic_slice_in_dim(member_order, start, BIG_DEV, 0)
            return masked_best(queries, query_ids, query_order, member_unit, member_ids, member_order)
        return lax.map(per_block, jnp.arange(CYCLE, dtype=jnp.int32)).reshape(group_rows)
    big_best = lax.map(per_group, grouped).reshape(BIG)
    return (small_best, big_best)
```

```python
import jax
import jax.numpy as jnp
from jax import lax
from jax.experimental import pallas as pl
from jax.experimental.pallas import tpu as pltpu
from jax.sharding import PartitionSpec as P

CYCLE = 16


def shifted(block, axis, distance):
    devices = range(lax.axis_size(axis))
    route = [((i - distance) % len(devices), i) for i in devices]
    return lax.ppermute(block, axis, route)


def unit_rows(matrix):
    widened = matrix.astype(jnp.float32)
    scaled = widened * lax.rsqrt(jnp.sum(widened * widened, axis=1, keepdims=True) + 1e-06)
    return scaled.astype(jnp.bfloat16)


def update_best(best_sim, queries, query_ids, query_order, keys_in, key_ids, key_order):
    sim_grid = lax.dot_general(
        queries, keys_in, (((1,), (1,)), ((), ())), preferred_element_type=jnp.float32
    )
    keep_mask = (query_ids[:, None] == key_ids[None, :]) & (
        key_order[None, :] < query_order[:, None]
    )
    return jnp.maximum(best_sim, jnp.max(jnp.where(keep_mask, sim_grid, -1.0), axis=1))


def both_ways(own_best, carried, own_rows, own_ids, own_order, block_rows, block_ids, block_order):
    sim_grid = lax.dot_general(
        own_rows, block_rows, (((1,), (1,)), ((), ())), preferred_element_type=jnp.float32
    )
    same_id = own_ids[:, None] == block_ids[None, :]
    own_mask = same_id & (block_order[None, :] < own_order[:, None])
    block_mask = same_id & (own_order[:, None] < block_order[None, :])
    own_best = jnp.maximum(own_best, jnp.max(jnp.where(own_mask, sim_grid, -1.0), axis=1))
    carried = jnp.maximum(carried, jnp.max(jnp.where(block_mask, sim_grid, -1.0), axis=0))
    return (own_best, carried)


def on_device(small_emb, small_cluster, small_index, big_emb, big_cluster, big_index):
    devices = lax.axis_size("blk")
    row_count = small_emb.shape[0]
    width = small_emb.shape[1]
    capacity = 2 * row_count // devices
    small_unit = unit_rows(small_emb)
    owner_of = small_cluster % devices
    one_hot = (owner_of[:, None] == jnp.arange(devices, dtype=jnp.int32)[None, :]).astype(jnp.int32)
    earlier = jnp.cumsum(one_hot, axis=0) - one_hot
    rank_in = jnp.sum(earlier * one_hot, axis=1)
    slot_of = owner_of * capacity + rank_in
    send_rows = (
        jnp.zeros((devices * capacity, width), jnp.bfloat16)
        .at[slot_of]
        .set(small_unit)
        .reshape(devices, capacity, width)
    )
    send_ids = (
        jnp.full((devices * capacity,), -1, jnp.int32)
        .at[slot_of]
        .set(small_cluster)
        .reshape(devices, capacity)
    )
    send_order = (
        jnp.zeros((devices * capacity,), jnp.int32)
        .at[slot_of]
        .set(small_index)
        .reshape(devices, capacity)
    )
    got_rows, got_ids, got_order = (
        lax.all_to_all(send_rows, "blk", split_axis=0, concat_axis=0, tiled=True),
        lax.all_to_all(send_ids, "blk", split_axis=0, concat_axis=0, tiled=True),
        lax.all_to_all(send_order, "blk", split_axis=0, concat_axis=0, tiled=True),
    )
    flat_rows = got_rows.reshape(devices * capacity, width)
    flat_ids = got_ids.reshape(devices * capacity)
    flat_order = got_order.reshape(devices * capacity)
    start_best = jnp.full((devices * capacity,), -1.0, jnp.float32)
    owner_best = update_best(
        start_best, flat_rows, flat_ids, flat_order, flat_rows, flat_ids, flat_order
    )
    returned = lax.all_to_all(
        owner_best.reshape(devices, capacity), "blk", split_axis=0, concat_axis=0, tiled=True
    )
    small_best = returned.reshape(devices * capacity)[slot_of]
    big_unit = unit_rows(big_emb)
    best_sim = jnp.full((big_unit.shape[0],), -1.0, jnp.float32)
    best_sim = update_best(
        best_sim, big_unit, big_cluster, big_index, big_unit, big_cluster, big_index
    )
    carried_start = jnp.full((big_unit.shape[0],), -1.0, jnp.float32)

    def one_turn(step_num, carry):
        running, block_rows, block_ids, block_order, carried = carry
        block_rows, block_ids, block_order = shifted((block_rows, block_ids, block_order), "blk", 1)
        carried = shifted(carried, "blk", 1)
        running, carried = both_ways(
            running, carried, big_unit, big_cluster, big_index, block_rows, block_ids, block_order
        )
        return (running, block_rows, block_ids, block_order, carried)

    final = lax.fori_loop(
        0, CYCLE - 1, one_turn, (best_sim, big_unit, big_cluster, big_index, carried_start)
    )
    home_gap = shifted(1.0 - final[4], "blk", -(CYCLE - 1))
    best_sim = jnp.maximum(final[0], 1.0 - home_gap)
    return (small_best, best_sim)


MESH = pl.DeviceIdType.MESH
META = 16
COLS = 256


class Side:
    def __init__(self, flip, emb, meta, out, buf, rowid, rowor, colmeta, accr, accc, fin, ret, ss, rs, fs, frs):
        self.emb, self.meta, self.out, self.buf = emb, meta, out, buf
        self.rowid, self.rowor, self.colmeta = rowid, rowor, colmeta
        self.accr, self.accc, self.fin, self.ret = accr, accc, fin, ret
        self.ss, self.rs, self.fs, self.frs = ss, rs, fs, frs
        self.flip = flip
        self.rows = emb.shape[0]
        self.parts = lax.axis_index("parts")
        b = lax.axis_index("blk")
        z = b // 4
        self.level = 3 - z if flip else z
        self.q = b % 4
        self.y, self.c = self.q // 2, self.q % 2

    def device(self, level, q):
        z = 3 - level if self.flip else level
        return (self.parts, z * 4 + q)

    def copy(self, src, dst, dev, sem):
        return pltpu.make_async_remote_copy(
            src_ref=self.buf.at[src], dst_ref=self.buf.at[dst], send_sem=self.ss.at[sem],
            recv_sem=self.rs.at[dst], device_id=dev, device_id_type=MESH,
        )

    def arrived(self, slot):
        self.copy(slot, slot, self.device(self.level, self.q ^ 1), 0).wait_recv()

    def plan(self):
        site = self.level % 2 == 0
        q, sib, opp = self.q, self.q ^ 1, self.q ^ 2
        here = self.level
        return {
            0: (site, q, q, self.device(here, sib)),
            1: (site, q, q, self.device(here, opp)),
            2: (site, opp, opp, self.device(here, sib)),
            3: (site, 4 + q, 4 + q, self.device(here, sib)),
            4: (site, 4 + q, 4 + q, self.device(here, opp)),
            5: (site, 4 + opp, 4 + opp, self.device(here, sib)),
            6: (here == 0, q, 9, self.device(2, q)),
            7: (here == 1, q, 8, self.device(2, q)),
            8: (~site, q, 4 + q, self.device(here - 1, q)),
        }

    def send(self, sem):
        cond, src, dst, dev = self.plan()[sem]

        @pl.when(cond)
        def _():
            self.copy(src, dst, dev, sem).start()

    def finish_sends(self):
        for sem, (cond, src, dst, dev) in self.plan().items():

            @pl.when(cond)
            def _():
                self.copy(src, dst, dev, sem).wait_send()

    def prepare(self):
        q = self.q
        rows = self.rows

        def step(t, _):
            r = pl.multiple_of(t * 128, 128)
            x = self.emb[pl.ds(r, 128), :].astype(jnp.float32)
            s = x * lax.rsqrt(jnp.sum(x * x, axis=1, keepdims=True) + 1e-06)
            self.buf[q, pl.ds(r, 128), :] = s.astype(jnp.bfloat16)
            return 0

        lax.fori_loop(0, rows // 128, step, 0)
        self.buf[q, rows : rows + META, :] = self.meta[...]

    def unpack(self, slot):
        rows = self.rows
        m = self.buf[slot, rows : rows + META, 0:rows].astype(jnp.float32)
        ids = m[0:1] * 256.0 + m[1:2]
        order = m[2:3] * 256.0 + m[3:4]
        self.colmeta[slot, 0:8, :] = jnp.broadcast_to(ids, (8, rows))
        self.colmeta[slot, 8:16, :] = jnp.broadcast_to(order, (8, rows))
        self.rowid[slot] = jnp.broadcast_to(ids, (128, rows)).T
        self.rowor[slot] = jnp.broadcast_to(order, (128, rows)).T
        self.accr[slot] = jnp.full((rows, 128), -1.0, jnp.float32)
        self.accc[slot] = jnp.full((8, rows), -1.0, jnp.float32)

    def pair(self, i, j, both=True):
        rows = self.rows
        left = self.buf[i, 0:rows, :]
        rid, ror = self.rowid[i], self.rowor[i]
        best = self.accr[i]
        for t in range(rows // COLS):
            right = self.buf[j, t * COLS : (t + 1) * COLS, :]
            sim = lax.dot_general(left, right, (((1,), (1,)), ((), ())), preferred_element_type=jnp.float32)
            for g in range(COLS // 128):
                at = t * COLS + g * 128
                s = sim[:, g * 128 : (g + 1) * 128]
                cid = self.colmeta[j, 0:1, at : at + 128]
                cor = self.colmeta[j, 8:9, at : at + 128]
                s = jnp.where(rid == cid, s, -1.0)
                before = cor < ror
                best = jnp.maximum(best, jnp.where(before, s, -1.0))
                if both:
                    back = jnp.where(before, -1.0, s).reshape(rows // 8, 8, 128)
                    self.accc[j, :, at : at + 128] = jnp.maximum(
                        self.accc[j, :, at : at + 128], jnp.max(back, axis=0)
                    )
        self.accr[i] = best

    def pairs(self, count, index):
        def step(n, _):
            i, j = index(n)
            self.pair(i, j)
            return 0

        lax.fori_loop(0, count, step, 0)

    def site_work(self):
        q, y, c = self.q, self.y, self.c
        sib, opp, far = q ^ 1, q ^ 2, q ^ 3
        crossed = self.level == 2
        self.unpack(q)
        self.pair(q, q, both=False)
        self.arrived(sib)
        self.unpack(sib)
        self.arrived(opp)
        self.send(2)
        self.send(6)
        self.arrived(4 + q)
        self.send(3)
        self.send(4)
        self.unpack(opp)
        self.unpack(4 + q)
        self.pair(4 + q, 4 + q, both=False)
        self.arrived(far)
        self.unpack(far)
        self.arrived(4 + sib)
        self.unpack(4 + sib)

        def early(n):
            i = jnp.where(n < 2, q, c * 4 + q)
            j = jnp.where(n == 0, 4 + q, jnp.where(n == 1, 4 + sib, c * 4 + sib))
            return i, j

        self.pairs(3, early)

        @pl.when(crossed)
        def _():
            self.arrived(8)
            self.unpack(8)
            self.pairs(6, lambda n: (8, jnp.where(n < 4, n, 4 + y * 2 + (n - 4))))

        self.arrived(4 + opp)
        self.send(5)
        self.unpack(4 + opp)
        self.arrived(4 + far)
        self.unpack(4 + far)

        def late(n):
            other = jnp.where(n % 2 == 0, opp, far)
            i = jnp.where(n < 2, q, y * 4 + q)
            j = jnp.where(n < 2, 4 + other, y * 4 + other)
            return i, j

        self.pairs(4, late)

        @pl.when(crossed)
        def _():
            self.pairs(2, lambda n: (8, 4 + (1 - y) * 2 + n))
            self.arrived(9)
            self.unpack(9)
            self.pairs(8, lambda n: (9, n))

        def close(k, _):
            self.close(k)

            @pl.when(k != q)
            def _():
                self.back(k).start()

            return 0

        lax.fori_loop(0, 8, close, 0)

        @pl.when(crossed)
        def _():
            for k in (8, 9):
                self.close(k)
                self.back_across(k).start()

        self.ret[q] = self.fin[q]

        def closed(k, _):
            @pl.when(k != q)
            def _():
                self.back(k).wait_send()

            return 0

        lax.fori_loop(0, 8, closed, 0)

        @pl.when(crossed)
        def _():
            for k in (8, 9):
                self.back_across(k).wait_send()

    def close(self, k):
        flat = self.accr[k].T.reshape(16, 8, self.rows)
        self.fin[k] = jnp.maximum(self.accc[k], jnp.max(flat, axis=0))

    def back(self, k):
        return self.back_to(k, self.q, self.device(self.level + k // 4, k % 4))

    def back_across(self, k):
        return self.back_to(k, 4, self.device(9 - k, self.q))

    def back_to(self, k, place, dev):
        return pltpu.make_async_remote_copy(
            src_ref=self.fin.at[k], dst_ref=self.ret.at[place], send_sem=self.fs.at[k],
            recv_sem=self.frs.at[place], device_id=dev, device_id_type=MESH,
        )

    def collect(self):
        site = self.level % 2 == 0
        first_half = self.level < 2

        @pl.when(~first_half)
        def _():
            self.ret[4] = jnp.full((8, self.rows), -1.0, jnp.float32)

        for p in range(4):

            @pl.when(~(site & (self.q == p)))
            def _():
                self.back_to(p, p, self.device(self.level, self.q ^ 1)).wait_recv()

        @pl.when(first_half)
        def _():
            self.back_to(4, 4, self.device(self.level, self.q ^ 1)).wait_recv()

        best = self.ret[4]
        for p in range(4):
            best = jnp.maximum(best, self.ret[p])
        self.out[...] = jnp.max(best, axis=0, keepdims=True)


def grid_kernel(be, bm, se, sm, bo, so, *scratch):
    half = len(scratch) // 2
    big = Side(False, be, bm, bo, *scratch[:half])
    small = Side(True, se, sm, so, *scratch[half:])
    me = lax.axis_index("blk")
    barrier = pltpu.get_barrier_semaphore()
    for d in range(1, CYCLE):
        peer = (big.parts, (me + d) % CYCLE)
        pl.semaphore_signal(barrier, inc=1, device_id=peer, device_id_type=MESH)
    big.prepare()
    small.prepare()
    pl.semaphore_wait(barrier, CYCLE - 1)
    for side in (big, small):
        side.send(0)
        side.send(1)
        side.send(7)
        side.send(8)
    for side in (big, small):
        pl.when(side.level % 2 == 0)(side.site_work)
    for side in (big, small):
        side.collect()
        side.finish_sends()


def side_scratch(rows, width):
    return [
        pltpu.VMEM((10, rows + META, width), jnp.bfloat16),
        pltpu.VMEM((10, rows, 128), jnp.float32),
        pltpu.VMEM((10, rows, 128), jnp.float32),
        pltpu.VMEM((10, 16, rows), jnp.float32),
        pltpu.VMEM((10, rows, 128), jnp.float32),
        pltpu.VMEM((10, 8, rows), jnp.float32),
        pltpu.VMEM((10, 8, rows), jnp.float32),
        pltpu.VMEM((5, 8, rows), jnp.float32),
        pltpu.SemaphoreType.DMA((9,)),
        pltpu.SemaphoreType.DMA((10,)),
        pltpu.SemaphoreType.DMA((10,)),
        pltpu.SemaphoreType.DMA((5,)),
    ]


def meta_rows(ids, order, width):
    rows = jnp.stack([ids // 256, ids % 256, order // 256, order % 256])
    return jnp.pad(rows, ((0, META - 4), (0, width - rows.shape[1]))).astype(jnp.bfloat16)


def on_square_grid(small_emb, small_cluster, small_index, big_emb, big_cluster, big_index):
    width = big_emb.shape[1]
    big_rows, small_rows = big_emb.shape[0], small_emb.shape[0]
    vmem = pl.BlockSpec(memory_space=pltpu.VMEM)
    big_best, small_best = pl.pallas_call(
        grid_kernel,
        out_shape=(
            jax.ShapeDtypeStruct((1, big_rows), jnp.float32),
            jax.ShapeDtypeStruct((1, small_rows), jnp.float32),
        ),
        in_specs=[vmem] * 4,
        out_specs=(vmem, vmem),
        scratch_shapes=side_scratch(big_rows, width) + side_scratch(small_rows, width),
        compiler_params=pltpu.CompilerParams(
            collective_id=0, has_side_effects=True, vmem_limit_bytes=48 << 20
        ),
    )(
        big_emb,
        meta_rows(big_cluster, big_index, width),
        small_emb,
        meta_rows(small_cluster, small_index, width),
    )
    return (small_best.reshape(small_rows), big_best.reshape(big_rows))


def solution(mesh):
    placed = (
        P(("parts", "blk"), None),
        P(("parts", "blk")),
        P(("parts", "blk")),
        P(("parts", "blk"), None),
        P(("parts", "blk")),
        P(("parts", "blk")),
    )
    return jax.shard_map(
        on_square_grid if mesh.shape["blk"] == CYCLE else on_device,
        mesh=mesh,
        in_specs=placed,
        out_specs=(P(("parts", "blk")), P(("parts", "blk"))),
        check_vma=False,
    )
```

```python
import jax
import jax.numpy as jnp
from jax import lax
from jax.experimental import pallas as pl
from jax.experimental.pallas import tpu as pltpu
from jax.sharding import PartitionSpec as P

CYCLE = 16


def shifted(block, axis, distance):
    devices = range(lax.axis_size(axis))
    route = [((i - distance) % len(devices), i) for i in devices]
    return lax.ppermute(block, axis, route)


def unit_rows(matrix):
    widened = matrix.astype(jnp.float32)
    scaled = widened * lax.rsqrt(jnp.sum(widened * widened, axis=1, keepdims=True) + 1e-06)
    return scaled.astype(jnp.bfloat16)


def update_best(best_sim, queries, query_ids, query_order, keys_in, key_ids, key_order):
    sim_grid = lax.dot_general(
        queries, keys_in, (((1,), (1,)), ((), ())), preferred_element_type=jnp.float32
    )
    keep_mask = (query_ids[:, None] == key_ids[None, :]) & (
        key_order[None, :] < query_order[:, None]
    )
    return jnp.maximum(best_sim, jnp.max(jnp.where(keep_mask, sim_grid, -1.0), axis=1))


def both_ways(own_best, carried, own_rows, own_ids, own_order, block_rows, block_ids, block_order):
    sim_grid = lax.dot_general(
        own_rows, block_rows, (((1,), (1,)), ((), ())), preferred_element_type=jnp.float32
    )
    same_id = own_ids[:, None] == block_ids[None, :]
    own_mask = same_id & (block_order[None, :] < own_order[:, None])
    block_mask = same_id & (own_order[:, None] < block_order[None, :])
    own_best = jnp.maximum(own_best, jnp.max(jnp.where(own_mask, sim_grid, -1.0), axis=1))
    carried = jnp.maximum(carried, jnp.max(jnp.where(block_mask, sim_grid, -1.0), axis=0))
    return (own_best, carried)


def on_device(small_emb, small_cluster, small_index, big_emb, big_cluster, big_index):
    devices = lax.axis_size("blk")
    row_count = small_emb.shape[0]
    width = small_emb.shape[1]
    capacity = 2 * row_count // devices
    small_unit = unit_rows(small_emb)
    owner_of = small_cluster % devices
    one_hot = (owner_of[:, None] == jnp.arange(devices, dtype=jnp.int32)[None, :]).astype(jnp.int32)
    earlier = jnp.cumsum(one_hot, axis=0) - one_hot
    rank_in = jnp.sum(earlier * one_hot, axis=1)
    slot_of = owner_of * capacity + rank_in
    send_rows = (
        jnp.zeros((devices * capacity, width), jnp.bfloat16)
        .at[slot_of]
        .set(small_unit)
        .reshape(devices, capacity, width)
    )
    send_ids = (
        jnp.full((devices * capacity,), -1, jnp.int32)
        .at[slot_of]
        .set(small_cluster)
        .reshape(devices, capacity)
    )
    send_order = (
        jnp.zeros((devices * capacity,), jnp.int32)
        .at[slot_of]
        .set(small_index)
        .reshape(devices, capacity)
    )
    got_rows, got_ids, got_order = (
        lax.all_to_all(send_rows, "blk", split_axis=0, concat_axis=0, tiled=True),
        lax.all_to_all(send_ids, "blk", split_axis=0, concat_axis=0, tiled=True),
        lax.all_to_all(send_order, "blk", split_axis=0, concat_axis=0, tiled=True),
    )
    flat_rows = got_rows.reshape(devices * capacity, width)
    flat_ids = got_ids.reshape(devices * capacity)
    flat_order = got_order.reshape(devices * capacity)
    start_best = jnp.full((devices * capacity,), -1.0, jnp.float32)
    owner_best = update_best(
        start_best, flat_rows, flat_ids, flat_order, flat_rows, flat_ids, flat_order
    )
    returned = lax.all_to_all(
        owner_best.reshape(devices, capacity), "blk", split_axis=0, concat_axis=0, tiled=True
    )
    small_best = returned.reshape(devices * capacity)[slot_of]
    big_unit = unit_rows(big_emb)
    best_sim = jnp.full((big_unit.shape[0],), -1.0, jnp.float32)
    best_sim = update_best(
        best_sim, big_unit, big_cluster, big_index, big_unit, big_cluster, big_index
    )
    carried_start = jnp.full((big_unit.shape[0],), -1.0, jnp.float32)

    def one_turn(step_num, carry):
        running, block_rows, block_ids, block_order, carried = carry
        block_rows, block_ids, block_order = shifted((block_rows, block_ids, block_order), "blk", 1)
        carried = shifted(carried, "blk", 1)
        running, carried = both_ways(
            running, carried, big_unit, big_cluster, big_index, block_rows, block_ids, block_order
        )
        return (running, block_rows, block_ids, block_order, carried)

    final = lax.fori_loop(
        0, CYCLE - 1, one_turn, (best_sim, big_unit, big_cluster, big_index, carried_start)
    )
    home_gap = shifted(1.0 - final[4], "blk", -(CYCLE - 1))
    best_sim = jnp.maximum(final[0], 1.0 - home_gap)
    return (small_best, best_sim)


MESH = pl.DeviceIdType.MESH
META = 16
COLS = 256


class Side:
    def __init__(self, flip, hbm, out, emb, ids, order, ls, buf, rowid, rowor, colmeta, accr, accc, fin, ret, ss, rs, fs, frs):
        self.hbm, self.loaded, self.ls, self.out, self.buf = hbm, (emb, ids, order), ls, out, buf
        self.emb = emb
        self.rowid, self.rowor, self.colmeta = rowid, rowor, colmeta
        self.accr, self.accc, self.fin, self.ret = accr, accc, fin, ret
        self.ss, self.rs, self.fs, self.frs = ss, rs, fs, frs
        self.flip = flip
        self.rows = emb.shape[0]
        self.parts = lax.axis_index("parts")
        b = lax.axis_index("blk")
        z = b // 4
        self.level = 3 - z if flip else z
        self.q = b % 4
        self.y, self.c = self.q // 2, self.q % 2

    def device(self, level, q):
        z = 3 - level if self.flip else level
        return (self.parts, z * 4 + q)

    def copy(self, src, dst, dev, sem):
        return pltpu.make_async_remote_copy(
            src_ref=self.buf.at[src], dst_ref=self.buf.at[dst], send_sem=self.ss.at[sem],
            recv_sem=self.rs.at[dst], device_id=dev, device_id_type=MESH,
        )

    def arrived(self, slot):
        self.copy(slot, slot, self.device(self.level, self.q ^ 1), 0).wait_recv()

    def plan(self):
        site = self.level % 2 == 0
        q, sib, opp = self.q, self.q ^ 1, self.q ^ 2
        here = self.level
        return {
            0: (site, q, q, self.device(here, sib)),
            1: (site, q, q, self.device(here, opp)),
            2: (site, opp, opp, self.device(here, sib)),
            3: (site, 4 + q, 4 + q, self.device(here, sib)),
            4: (site, 4 + q, 4 + q, self.device(here, opp)),
            5: (site, 4 + opp, 4 + opp, self.device(here, sib)),
            6: (here == 0, q, 9, self.device(2, q)),
            7: (here == 1, q, 8, self.device(2, q)),
            8: (~site, q, 4 + q, self.device(here - 1, q)),
        }

    def send(self, sem):
        cond, src, dst, dev = self.plan()[sem]

        @pl.when(cond)
        def _():
            self.copy(src, dst, dev, sem).start()

    def finish_sends(self):
        for sem, (cond, src, dst, dev) in self.plan().items():

            @pl.when(cond)
            def _():
                self.copy(src, dst, dev, sem).wait_send()

    def loads(self):
        return [pltpu.make_async_copy(h, v, self.ls.at[k]) for k, (h, v) in enumerate(zip(self.hbm, self.loaded))]

    def prepare(self):
        q = self.q
        rows = self.rows
        for load in self.loads():
            load.wait()

        def step(t, _):
            r = pl.multiple_of(t * 128, 128)
            x = self.emb[pl.ds(r, 128), :].astype(jnp.float32)
            s = x * lax.rsqrt(jnp.sum(x * x, axis=1, keepdims=True) + 1e-06)
            self.buf[q, pl.ds(r, 128), :] = s.astype(jnp.bfloat16)
            return 0

        lax.fori_loop(0, rows // 128, step, 0)
        ids = jnp.broadcast_to(self.loaded[1][...].reshape(1, rows), (META, rows))
        order = jnp.broadcast_to(self.loaded[2][...].reshape(1, rows), (META, rows))
        line = lax.broadcasted_iota(jnp.int32, (META, rows), 0)
        both = jnp.where(line < 2, ids, order)
        digits = jnp.where(line % 2 == 0, both >> 8, both & 255)
        digits = jnp.where(line < 4, digits, 0).astype(jnp.float32)
        self.buf[q, rows : rows + META, 0:rows] = digits.astype(jnp.bfloat16)
        self.buf[q, rows : rows + META, rows:] = jnp.zeros((META, self.buf.shape[2] - rows), jnp.bfloat16)

    def unpack(self, slot, left=True):
        rows = self.rows
        m = self.buf[slot, rows : rows + META, 0:rows].astype(jnp.float32)
        ids = m[0:1] * 256.0 + m[1:2]
        order = m[2:3] * 256.0 + m[3:4]
        self.colmeta[slot, 0:8, :] = jnp.broadcast_to(ids, (8, rows))
        self.colmeta[slot, 8:16, :] = jnp.broadcast_to(order, (8, rows))
        self.accc[slot] = jnp.full((8, rows), -1.0, jnp.float32)
        if not left:
            return
        self.rowid[slot] = jnp.broadcast_to(ids, (128, rows)).T
        self.rowor[slot] = jnp.broadcast_to(order, (128, rows)).T
        self.accr[slot] = jnp.full((rows, 128), -1.0, jnp.float32)

    def pair(self, i, j, both=True):
        rows = self.rows
        left = self.buf[i, 0:rows, :]
        rid, ror = self.rowid[i], self.rowor[i]
        best = self.accr[i]
        for t in range(rows // COLS):
            right = self.buf[j, t * COLS : (t + 1) * COLS, :]
            sim = lax.dot_general(left, right, (((1,), (1,)), ((), ())), preferred_element_type=jnp.float32)
            for g in range(COLS // 128):
                at = t * COLS + g * 128
                s = sim[:, g * 128 : (g + 1) * 128]
                cid = self.colmeta[j, 0:1, at : at + 128]
                cor = self.colmeta[j, 8:9, at : at + 128]
                s = jnp.where(rid == cid, s, -1.0)
                before = cor < ror
                best = jnp.maximum(best, jnp.where(before, s, -1.0))
                if both:
                    back = jnp.where(before, -1.0, s).reshape(rows // 8, 8, 128)
                    self.accc[j, :, at : at + 128] = jnp.maximum(
                        self.accc[j, :, at : at + 128], jnp.max(back, axis=0)
                    )
        self.accr[i] = best

    def pairs(self, count, index):
        def step(n, _):
            i, j = index(n)
            self.pair(i, j)
            return 0

        lax.fori_loop(0, count, step, 0)

    def site_work(self):
        q, y, c = self.q, self.y, self.c
        sib, opp, far = q ^ 1, q ^ 2, q ^ 3
        crossed = self.level == 2
        self.unpack(q)
        self.pair(q, q, both=False)
        self.arrived(sib)
        self.unpack(sib, left=False)
        self.arrived(opp)
        self.send(2)
        self.send(6)
        self.arrived(4 + q)
        self.send(3)
        self.send(4)
        self.unpack(opp, left=False)
        self.unpack(4 + q)
        self.pair(4 + q, 4 + q, both=False)
        self.arrived(far)
        self.unpack(far, left=False)
        self.arrived(4 + sib)
        self.unpack(4 + sib, left=False)

        def early(n):
            i = jnp.where(n < 2, q, c * 4 + q)
            j = jnp.where(n == 0, 4 + q, jnp.where(n == 1, 4 + sib, c * 4 + sib))
            return i, j

        self.pairs(3, early)

        @pl.when(crossed)
        def _():
            self.arrived(8)
            self.unpack(8)
            self.pairs(6, lambda n: (8, jnp.where(n < 4, n, 4 + y * 2 + (n - 4))))

        self.arrived(4 + opp)
        self.send(5)
        self.unpack(4 + opp, left=False)

        @pl.when(crossed)
        def _():
            self.arrived(9)
            self.unpack(9)
            self.pairs(6, lambda n: (9, jnp.where(n < 4, n, 4 + y * 2 + (n - 4))))

        self.arrived(4 + far)
        self.unpack(4 + far, left=False)

        def late(n):
            other = jnp.where(n % 2 == 0, opp, far)
            i = jnp.where(n < 2, q, y * 4 + q)
            j = jnp.where(n < 2, 4 + other, y * 4 + other)
            return i, j

        self.pairs(4, late)

        @pl.when(crossed)
        def _():
            self.pairs(4, lambda n: (8 + n // 2, 4 + (1 - y) * 2 + n % 2))

        def close(k, _):
            left = (k == q) | (k == 4 + q)

            @pl.when(~left)
            def _():
                self.fin[k] = self.accc[k]

            @pl.when(left)
            def _():
                self.close(k)

            @pl.when(k != q)
            def _():
                self.back(k).start()

            return 0

        lax.fori_loop(0, 8, close, 0)

        @pl.when(crossed)
        def _():
            for k in (8, 9):
                self.close(k)
                self.back_across(k).start()

        self.ret[q] = self.fin[q]

        def closed(k, _):
            @pl.when(k != q)
            def _():
                self.back(k).wait_send()

            return 0

        lax.fori_loop(0, 8, closed, 0)

        @pl.when(crossed)
        def _():
            for k in (8, 9):
                self.back_across(k).wait_send()

    def close(self, k):
        flat = self.accr[k].T.reshape(16, 8, self.rows)
        self.fin[k] = jnp.maximum(self.accc[k], jnp.max(flat, axis=0))

    def back(self, k):
        return self.back_to(k, self.q, self.device(self.level + k // 4, k % 4))

    def back_across(self, k):
        return self.back_to(k, 4, self.device(9 - k, self.q))

    def back_to(self, k, place, dev):
        return pltpu.make_async_remote_copy(
            src_ref=self.fin.at[k], dst_ref=self.ret.at[place], send_sem=self.fs.at[k],
            recv_sem=self.frs.at[place], device_id=dev, device_id_type=MESH,
        )

    def collect(self):
        site = self.level % 2 == 0
        first_half = self.level < 2

        @pl.when(~first_half)
        def _():
            self.ret[4] = jnp.full((8, self.rows), -1.0, jnp.float32)

        for p in range(4):

            @pl.when(~(site & (self.q == p)))
            def _():
                self.back_to(p, p, self.device(self.level, self.q ^ 1)).wait_recv()

        @pl.when(first_half)
        def _():
            self.back_to(4, 4, self.device(self.level, self.q ^ 1)).wait_recv()

        best = self.ret[4]
        for p in range(4):
            best = jnp.maximum(best, self.ret[p])
        self.out[...] = jnp.max(best, axis=0)


def grid_kernel(be, bc, bi, se, sc, si, bo, so, *scratch):
    half = len(scratch) // 2
    big = Side(False, (be, bc, bi), bo, *scratch[:half])
    small = Side(True, (se, sc, si), so, *scratch[half:])
    me = lax.axis_index("blk")
    barrier = pltpu.get_barrier_semaphore()
    for d in range(1, CYCLE):
        peer = (big.parts, (me + d) % CYCLE)
        pl.semaphore_signal(barrier, inc=1, device_id=peer, device_id_type=MESH)
    for side in (big, small):
        for load in side.loads():
            load.start()
    big.prepare()
    pl.semaphore_wait(barrier, CYCLE - 1)
    for sem in (8, 7, 1, 0):
        big.send(sem)
    small.prepare()
    for sem in (8, 7, 1, 0):
        small.send(sem)
    for side in (big, small):
        pl.when(side.level % 2 == 0)(side.site_work)
    for side in (big, small):
        side.collect()
        side.finish_sends()


def side_scratch(rows, width):
    return [
        pltpu.VMEM((rows, width), jnp.bfloat16),
        pltpu.VMEM((rows,), jnp.int32),
        pltpu.VMEM((rows,), jnp.int32),
        pltpu.SemaphoreType.DMA((3,)),
        pltpu.VMEM((10, rows + META, width), jnp.bfloat16),
        pltpu.VMEM((10, rows, 128), jnp.float32),
        pltpu.VMEM((10, rows, 128), jnp.float32),
        pltpu.VMEM((10, 16, rows), jnp.float32),
        pltpu.VMEM((10, rows, 128), jnp.float32),
        pltpu.VMEM((10, 8, rows), jnp.float32),
        pltpu.VMEM((10, 8, rows), jnp.float32),
        pltpu.VMEM((5, 8, rows), jnp.float32),
        pltpu.SemaphoreType.DMA((9,)),
        pltpu.SemaphoreType.DMA((10,)),
        pltpu.SemaphoreType.DMA((10,)),
        pltpu.SemaphoreType.DMA((5,)),
    ]


def on_square_grid(small_emb, small_cluster, small_index, big_emb, big_cluster, big_index):
    width = big_emb.shape[1]
    big_rows, small_rows = big_emb.shape[0], small_emb.shape[0]
    vmem = pl.BlockSpec(memory_space=pltpu.VMEM)
    big_best, small_best = pl.pallas_call(
        grid_kernel,
        out_shape=(
            jax.ShapeDtypeStruct((big_rows,), jnp.float32),
            jax.ShapeDtypeStruct((small_rows,), jnp.float32),
        ),
        in_specs=[pl.BlockSpec(memory_space=pl.ANY)] * 6,
        out_specs=(vmem, vmem),
        scratch_shapes=side_scratch(big_rows, width) + side_scratch(small_rows, width),
        compiler_params=pltpu.CompilerParams(
            collective_id=0, has_side_effects=True, vmem_limit_bytes=60 << 20
        ),
    )(big_emb, big_cluster, big_index, small_emb, small_cluster, small_index)
    return (small_best, big_best)


def solution(mesh):
    placed = (
        P(("parts", "blk"), None),
        P(("parts", "blk")),
        P(("parts", "blk")),
        P(("parts", "blk"), None),
        P(("parts", "blk")),
        P(("parts", "blk")),
    )
    return jax.shard_map(
        on_square_grid if mesh.shape["blk"] == CYCLE else on_device,
        mesh=mesh,
        in_specs=placed,
        out_specs=(P(("parts", "blk")), P(("parts", "blk"))),
        check_vma=False,
    )
```

```python
import jax
import jax.numpy as jnp
from jax import lax
from jax.experimental import pallas as pl
from jax.experimental.pallas import tpu as pltpu
from jax.sharding import PartitionSpec as P

CYCLE = 16


def shifted(block, axis, distance):
    devices = range(lax.axis_size(axis))
    route = [((i - distance) % len(devices), i) for i in devices]
    return lax.ppermute(block, axis, route)


def unit_rows(matrix):
    widened = matrix.astype(jnp.float32)
    scaled = widened * lax.rsqrt(jnp.sum(widened * widened, axis=1, keepdims=True) + 1e-06)
    return scaled.astype(jnp.bfloat16)


def update_best(best_sim, queries, query_ids, query_order, keys_in, key_ids, key_order):
    sim_grid = lax.dot_general(
        queries, keys_in, (((1,), (1,)), ((), ())), preferred_element_type=jnp.float32
    )
    keep_mask = (query_ids[:, None] == key_ids[None, :]) & (
        key_order[None, :] < query_order[:, None]
    )
    return jnp.maximum(best_sim, jnp.max(jnp.where(keep_mask, sim_grid, -1.0), axis=1))


def both_ways(own_best, carried, own_rows, own_ids, own_order, block_rows, block_ids, block_order):
    sim_grid = lax.dot_general(
        own_rows, block_rows, (((1,), (1,)), ((), ())), preferred_element_type=jnp.float32
    )
    same_id = own_ids[:, None] == block_ids[None, :]
    own_mask = same_id & (block_order[None, :] < own_order[:, None])
    block_mask = same_id & (own_order[:, None] < block_order[None, :])
    own_best = jnp.maximum(own_best, jnp.max(jnp.where(own_mask, sim_grid, -1.0), axis=1))
    carried = jnp.maximum(carried, jnp.max(jnp.where(block_mask, sim_grid, -1.0), axis=0))
    return (own_best, carried)


def on_device(small_emb, small_cluster, small_index, big_emb, big_cluster, big_index):
    devices = lax.axis_size("blk")
    row_count = small_emb.shape[0]
    width = small_emb.shape[1]
    capacity = 2 * row_count // devices
    small_unit = unit_rows(small_emb)
    owner_of = small_cluster % devices
    one_hot = (owner_of[:, None] == jnp.arange(devices, dtype=jnp.int32)[None, :]).astype(jnp.int32)
    earlier = jnp.cumsum(one_hot, axis=0) - one_hot
    rank_in = jnp.sum(earlier * one_hot, axis=1)
    slot_of = owner_of * capacity + rank_in
    send_rows = (
        jnp.zeros((devices * capacity, width), jnp.bfloat16)
        .at[slot_of]
        .set(small_unit)
        .reshape(devices, capacity, width)
    )
    send_ids = (
        jnp.full((devices * capacity,), -1, jnp.int32)
        .at[slot_of]
        .set(small_cluster)
        .reshape(devices, capacity)
    )
    send_order = (
        jnp.zeros((devices * capacity,), jnp.int32)
        .at[slot_of]
        .set(small_index)
        .reshape(devices, capacity)
    )
    got_rows, got_ids, got_order = (
        lax.all_to_all(send_rows, "blk", split_axis=0, concat_axis=0, tiled=True),
        lax.all_to_all(send_ids, "blk", split_axis=0, concat_axis=0, tiled=True),
        lax.all_to_all(send_order, "blk", split_axis=0, concat_axis=0, tiled=True),
    )
    flat_rows = got_rows.reshape(devices * capacity, width)
    flat_ids = got_ids.reshape(devices * capacity)
    flat_order = got_order.reshape(devices * capacity)
    start_best = jnp.full((devices * capacity,), -1.0, jnp.float32)
    owner_best = update_best(
        start_best, flat_rows, flat_ids, flat_order, flat_rows, flat_ids, flat_order
    )
    returned = lax.all_to_all(
        owner_best.reshape(devices, capacity), "blk", split_axis=0, concat_axis=0, tiled=True
    )
    small_best = returned.reshape(devices * capacity)[slot_of]
    big_unit = unit_rows(big_emb)
    best_sim = jnp.full((big_unit.shape[0],), -1.0, jnp.float32)
    best_sim = update_best(
        best_sim, big_unit, big_cluster, big_index, big_unit, big_cluster, big_index
    )
    carried_start = jnp.full((big_unit.shape[0],), -1.0, jnp.float32)

    def one_turn(step_num, carry):
        running, block_rows, block_ids, block_order, carried = carry
        block_rows, block_ids, block_order = shifted((block_rows, block_ids, block_order), "blk", 1)
        carried = shifted(carried, "blk", 1)
        running, carried = both_ways(
            running, carried, big_unit, big_cluster, big_index, block_rows, block_ids, block_order
        )
        return (running, block_rows, block_ids, block_order, carried)

    final = lax.fori_loop(
        0, CYCLE - 1, one_turn, (best_sim, big_unit, big_cluster, big_index, carried_start)
    )
    home_gap = shifted(1.0 - final[4], "blk", -(CYCLE - 1))
    best_sim = jnp.maximum(final[0], 1.0 - home_gap)
    return (small_best, best_sim)


MESH = pl.DeviceIdType.MESH
META = 16
COLS = 512


class Side:
    def __init__(self, flip, hbm, out, emb, ids, order, ls, buf, rowid, rowor, colmeta, accr, accc, fin, ret, ss, rs, fs, frs):
        self.hbm, self.loaded, self.ls, self.out, self.buf = hbm, (emb, ids, order), ls, out, buf
        self.emb = emb
        self.rowid, self.rowor, self.colmeta = rowid, rowor, colmeta
        self.accr, self.accc, self.fin, self.ret = accr, accc, fin, ret
        self.ss, self.rs, self.fs, self.frs = ss, rs, fs, frs
        self.flip = flip
        self.rows = emb.shape[0]
        self.parts = lax.axis_index("parts")
        b = lax.axis_index("blk")
        z = b // 4
        self.level = 3 - z if flip else z
        self.q = b % 4
        self.y, self.c = self.q // 2, self.q % 2

    def device(self, level, q):
        z = 3 - level if self.flip else level
        return (self.parts, z * 4 + q)

    def copy(self, src, dst, dev, sem):
        return pltpu.make_async_remote_copy(
            src_ref=self.buf.at[src], dst_ref=self.buf.at[dst], send_sem=self.ss.at[sem],
            recv_sem=self.rs.at[dst], device_id=dev, device_id_type=MESH,
        )

    def arrived(self, slot):
        self.copy(slot, slot, self.device(self.level, self.q ^ 1), 0).wait_recv()

    def plan(self):
        site = self.level % 2 == 0
        q, sib, opp = self.q, self.q ^ 1, self.q ^ 2
        here = self.level
        return {
            0: (site, q, q, self.device(here, sib)),
            1: (site, q, q, self.device(here, opp)),
            2: (site, opp, opp, self.device(here, sib)),
            3: (site, 4 + q, 4 + q, self.device(here, sib)),
            4: (site, 4 + q, 4 + q, self.device(here, opp)),
            5: (site, 4 + opp, 4 + opp, self.device(here, sib)),
            6: (here == 0, q, 9, self.device(2, q)),
            7: (here == 1, q, 8, self.device(2, q)),
            8: (~site, q, 4 + q, self.device(here - 1, q)),
        }

    def send(self, sem):
        cond, src, dst, dev = self.plan()[sem]

        @pl.when(cond)
        def _():
            self.copy(src, dst, dev, sem).start()

    def finish_sends(self):
        for sem, (cond, src, dst, dev) in self.plan().items():

            @pl.when(cond)
            def _():
                self.copy(src, dst, dev, sem).wait_send()

    def loads(self):
        return [pltpu.make_async_copy(h, v, self.ls.at[k]) for k, (h, v) in enumerate(zip(self.hbm, self.loaded))]

    def prepare(self):
        q = self.q
        rows = self.rows
        for load in self.loads():
            load.wait()

        def step(t, _):
            r = pl.multiple_of(t * 128, 128)
            x = self.emb[pl.ds(r, 128), :].astype(jnp.float32)
            s = x * lax.rsqrt(jnp.sum(x * x, axis=1, keepdims=True) + 1e-06)
            self.buf[q, pl.ds(r, 128), :] = s.astype(jnp.bfloat16)
            return 0

        lax.fori_loop(0, rows // 128, step, 0)
        ids = jnp.broadcast_to(self.loaded[1][...].reshape(1, rows), (META, rows))
        order = jnp.broadcast_to(self.loaded[2][...].reshape(1, rows), (META, rows))
        line = lax.broadcasted_iota(jnp.int32, (META, rows), 0)
        both = jnp.where(line < 2, ids, order)
        digits = jnp.where(line % 2 == 0, both >> 8, both & 255)
        digits = jnp.where(line < 4, digits, 0).astype(jnp.float32)
        self.buf[q, rows : rows + META, 0:rows] = digits.astype(jnp.bfloat16)
        self.buf[q, rows : rows + META, rows:] = jnp.zeros((META, self.buf.shape[2] - rows), jnp.bfloat16)

    def unpack(self, slot, left=True):
        rows = self.rows
        m = self.buf[slot, rows : rows + META, 0:rows].astype(jnp.float32)
        ids = m[0:1] * 256.0 + m[1:2]
        order = m[2:3] * 256.0 + m[3:4]
        self.colmeta[slot, 0:8, :] = jnp.broadcast_to(ids, (8, rows))
        self.colmeta[slot, 8:16, :] = jnp.broadcast_to(order, (8, rows))
        self.accc[slot] = jnp.full((8, rows), -1.0, jnp.float32)
        if not left:
            return
        self.rowid[slot] = jnp.broadcast_to(ids, (128, rows)).T
        self.rowor[slot] = jnp.broadcast_to(order, (128, rows)).T
        self.accr[slot] = jnp.full((rows, 128), -1.0, jnp.float32)

    def pair(self, i, j, both=True):
        rows = self.rows
        cols = min(COLS, rows)
        left = self.buf[i, 0:rows, :]
        rid, ror = self.rowid[i], self.rowor[i]
        best = self.accr[i]
        for t in range(rows // cols):
            right = self.buf[j, t * cols : (t + 1) * cols, :]
            sim = lax.dot_general(left, right, (((1,), (1,)), ((), ())), preferred_element_type=jnp.float32)
            for g in range(cols // 128):
                at = t * cols + g * 128
                s = sim[:, g * 128 : (g + 1) * 128]
                cid = self.colmeta[j, 0:1, at : at + 128]
                cor = self.colmeta[j, 8:9, at : at + 128]
                s = jnp.where(rid == cid, s, -1.0)
                before = cor < ror
                best = jnp.maximum(best, jnp.where(before, s, -1.0))
                if both:
                    back = jnp.where(before, -1.0, s).reshape(rows // 8, 8, 128)
                    self.accc[j, :, at : at + 128] = jnp.maximum(
                        self.accc[j, :, at : at + 128], jnp.max(back, axis=0)
                    )
        self.accr[i] = best

    def pairs(self, count, index):
        def step(n, _):
            i, j = index(n)
            self.pair(i, j)
            return 0

        lax.fori_loop(0, count, step, 0)

    def site_work(self):
        q, y, c = self.q, self.y, self.c
        sib, opp, far = q ^ 1, q ^ 2, q ^ 3
        crossed = self.level == 2
        self.unpack(q)
        self.pair(q, q, both=False)
        self.arrived(sib)
        self.unpack(sib, left=False)
        self.arrived(opp)
        self.send(2)
        self.send(6)
        self.arrived(4 + q)
        self.send(3)
        self.send(4)
        self.unpack(opp, left=False)
        self.unpack(4 + q)
        self.pair(4 + q, 4 + q, both=False)
        self.arrived(far)
        self.unpack(far, left=False)
        self.arrived(4 + sib)
        self.unpack(4 + sib, left=False)

        def early(n):
            i = jnp.where(n < 2, q, c * 4 + q)
            j = jnp.where(n == 0, 4 + q, jnp.where(n == 1, 4 + sib, c * 4 + sib))
            return i, j

        self.pairs(3, early)

        @pl.when(crossed)
        def _():
            self.arrived(8)
            self.unpack(8)
            self.pairs(6, lambda n: (8, jnp.where(n < 4, n, 4 + y * 2 + (n - 4))))

        self.arrived(4 + opp)
        self.send(5)
        self.unpack(4 + opp, left=False)

        @pl.when(crossed)
        def _():
            self.arrived(9)
            self.unpack(9)
            self.pairs(6, lambda n: (9, jnp.where(n < 4, n, 4 + y * 2 + (n - 4))))

        self.arrived(4 + far)
        self.unpack(4 + far, left=False)

        def late(n):
            other = jnp.where(n % 2 == 0, opp, far)
            i = jnp.where(n < 2, q, y * 4 + q)
            j = jnp.where(n < 2, 4 + other, y * 4 + other)
            return i, j

        self.pairs(4, late)

        @pl.when(crossed)
        def _():
            self.pairs(4, lambda n: (8 + n // 2, 4 + (1 - y) * 2 + n % 2))

        def close(k, _):
            left = (k == q) | (k == 4 + q)

            @pl.when(~left)
            def _():
                self.fin[k] = self.accc[k]

            @pl.when(left)
            def _():
                self.close(k)

            @pl.when(k != q)
            def _():
                self.back(k).start()

            return 0

        lax.fori_loop(0, 8, close, 0)

        @pl.when(crossed)
        def _():
            for k in (8, 9):
                self.close(k)
                self.back_across(k).start()

        self.ret[q] = self.fin[q]

        def closed(k, _):
            @pl.when(k != q)
            def _():
                self.back(k).wait_send()

            return 0

        lax.fori_loop(0, 8, closed, 0)

        @pl.when(crossed)
        def _():
            for k in (8, 9):
                self.back_across(k).wait_send()

    def close(self, k):
        flat = self.accr[k].T.reshape(16, 8, self.rows)
        self.fin[k] = jnp.maximum(self.accc[k], jnp.max(flat, axis=0))

    def back(self, k):
        return self.back_to(k, self.q, self.device(self.level + k // 4, k % 4))

    def back_across(self, k):
        return self.back_to(k, 4, self.device(9 - k, self.q))

    def back_to(self, k, place, dev):
        return pltpu.make_async_remote_copy(
            src_ref=self.fin.at[k], dst_ref=self.ret.at[place], send_sem=self.fs.at[k],
            recv_sem=self.frs.at[place], device_id=dev, device_id_type=MESH,
        )

    def collect(self):
        site = self.level % 2 == 0
        first_half = self.level < 2

        @pl.when(~first_half)
        def _():
            self.ret[4] = jnp.full((8, self.rows), -1.0, jnp.float32)

        for p in range(4):

            @pl.when(~(site & (self.q == p)))
            def _():
                self.back_to(p, p, self.device(self.level, self.q ^ 1)).wait_recv()

        @pl.when(first_half)
        def _():
            self.back_to(4, 4, self.device(self.level, self.q ^ 1)).wait_recv()

        best = self.ret[4]
        for p in range(4):
            best = jnp.maximum(best, self.ret[p])
        self.out[...] = jnp.max(best, axis=0)


def grid_kernel(be, bc, bi, se, sc, si, bo, so, *scratch):
    half = len(scratch) // 2
    big = Side(False, (be, bc, bi), bo, *scratch[:half])
    small = Side(True, (se, sc, si), so, *scratch[half:])
    me = lax.axis_index("blk")
    barrier = pltpu.get_barrier_semaphore()
    for d in range(1, CYCLE):
        peer = (big.parts, (me + d) % CYCLE)
        pl.semaphore_signal(barrier, inc=1, device_id=peer, device_id_type=MESH)
    for side in (big, small):
        for load in side.loads():
            load.start()
    big.prepare()
    pl.semaphore_wait(barrier, CYCLE - 1)
    for sem in (8, 7, 1, 0):
        big.send(sem)
    small.prepare()
    for sem in (8, 7, 1, 0):
        small.send(sem)
    for side in (big, small):
        pl.when(side.level % 2 == 0)(side.site_work)
    for side in (big, small):
        side.collect()
        side.finish_sends()


def side_scratch(rows, width):
    return [
        pltpu.VMEM((rows, width), jnp.bfloat16),
        pltpu.VMEM((rows,), jnp.int32),
        pltpu.VMEM((rows,), jnp.int32),
        pltpu.SemaphoreType.DMA((3,)),
        pltpu.VMEM((10, rows + META, width), jnp.bfloat16),
        pltpu.VMEM((10, rows, 128), jnp.float32),
        pltpu.VMEM((10, rows, 128), jnp.float32),
        pltpu.VMEM((10, 16, rows), jnp.float32),
        pltpu.VMEM((10, rows, 128), jnp.float32),
        pltpu.VMEM((10, 8, rows), jnp.float32),
        pltpu.VMEM((10, 8, rows), jnp.float32),
        pltpu.VMEM((5, 8, rows), jnp.float32),
        pltpu.SemaphoreType.DMA((9,)),
        pltpu.SemaphoreType.DMA((10,)),
        pltpu.SemaphoreType.DMA((10,)),
        pltpu.SemaphoreType.DMA((5,)),
    ]


def on_square_grid(small_emb, small_cluster, small_index, big_emb, big_cluster, big_index):
    width = big_emb.shape[1]
    big_rows, small_rows = big_emb.shape[0], small_emb.shape[0]
    vmem = pl.BlockSpec(memory_space=pltpu.VMEM)
    big_best, small_best = pl.pallas_call(
        grid_kernel,
        out_shape=(
            jax.ShapeDtypeStruct((big_rows,), jnp.float32),
            jax.ShapeDtypeStruct((small_rows,), jnp.float32),
        ),
        in_specs=[pl.BlockSpec(memory_space=pl.ANY)] * 6,
        out_specs=(vmem, vmem),
        scratch_shapes=side_scratch(big_rows, width) + side_scratch(small_rows, width),
        compiler_params=pltpu.CompilerParams(
            collective_id=0, has_side_effects=True, vmem_limit_bytes=60 << 20
        ),
    )(big_emb, big_cluster, big_index, small_emb, small_cluster, small_index)
    return (small_best, big_best)


def solution(mesh):
    placed = (
        P(("parts", "blk"), None),
        P(("parts", "blk")),
        P(("parts", "blk")),
        P(("parts", "blk"), None),
        P(("parts", "blk")),
        P(("parts", "blk")),
    )
    return jax.shard_map(
        on_square_grid if mesh.shape["blk"] == CYCLE else on_device,
        mesh=mesh,
        in_specs=placed,
        out_specs=(P(("parts", "blk")), P(("parts", "blk"))),
        check_vma=False,
    )
```
